32 devices in a mesh: lat: 4 (over y, x), lon: 2 (over core), ch: 4 (over z).
Axes of the slice: x: 2, y: 2, z: 4, core: 2. Of those that a mesh axis runs over, the one named last changes fastest.
Arguments:
- features: bfloat16 [1, 64, 128, 256], P(None, 'lat', 'lon'), may hold values from -6 to 6
- w_first: bfloat16 [5, 5, 256, 256], P(None, None, None, 'ch'), may hold values from -0.078125 to 0.078125
- bias_first: float32 [256], P('ch'), may hold values from -3 to 3
- w_second: bfloat16 [5, 5, 256, 256], P(None, None, 'ch'), may hold values from -0.109375 to 0.109375
- bias_second: float32 [256], replicated, may hold values from -3 to 3
- norm_gain: float32 [256], replicated, may hold values from 0.25 to 1.75
- norm_shift: float32 [256], replicated, may hold values from -3 to 3
- w_down: bfloat16 [2, 2, 256, 256], P(None, None, None, 'ch'), may hold values from -0.1875 to 0.1875
- bias_down: float32 [256], P('ch'), may hold values from -3 to 3
Outputs:
- downsampled: bfloat16 [1, 32, 64, 256], P(None, 'lat', 'lon', 'ch')
The draws below stay inside these ranges and needn't reach their ends.
All inputs are finite; a program needn't handle non-finite values.
Results may differ from the reference program's by a relative error of at most 0.011.
Values may be sent and summed in bfloat16 or wider, within the bound.
A program may use at most 64 MiB of HBM per device.

```python
import jax
import jax.numpy as jnp
from jax import lax

C = 256
BATCH = 1
H = 64
W = 128
N_CH = 4


def spiked(values, rng, source, target, parts, factor):
    def block_of(axis_at):
        return (jnp.arange(values.shape[axis_at]) // (values.shape[axis_at] // parts)).reshape((-1,) + (1,) * (values.ndim - 1 - axis_at))

    near = jax.random.permutation(rng, parts)[block_of(target)]
    far = (block_of(target) + parts // 2) % parts
    return jnp.where((block_of(source) == near) | (block_of(source) == far), factor * values, values)


def steps_of(own_key, extent, cuts, least, high):
    def one(position, shards_of):
        steps = jax.random.uniform(jax.random.fold_in(jax.random.fold_in(own_key, 6), position), (shards_of,), jnp.float32, least / len(cuts), high / len(cuts))
        return jnp.repeat(jnp.exp(steps), extent[position] // shards_of).reshape((-1,) + (1,) * (len(extent) - position - 1))

    loudness = one(*cuts[0])
    for cut in cuts[1:]:
        loudness = loudness * one(*cut)
    return loudness


def normal_values(own_key, shape, spread, reach, pieces=(), held_as=jnp.bfloat16):
    level = steps_of(own_key, shape, pieces, -0.22, 0.18) if pieces else 1.0
    drawn = jax.random.normal(own_key, shape, jnp.float32) * spread * level
    return jnp.minimum(jnp.maximum(drawn, -reach), reach).astype(held_as)


def heavy_noise(stream_key, dims, width, reach, pieces, heavy, dtype=jnp.bfloat16):
    values = width * jax.random.normal(stream_key, dims, jnp.float32)
    if pieces:
        values = values * steps_of(stream_key, dims, pieces, -0.22, 0.18)
    return jnp.clip(spiked(values, jax.random.fold_in(stream_key, 3), *heavy), -reach, reach).astype(dtype)


def setup_inputs(seed: int = 0) -> dict:
    key_list = jax.random.split(jax.random.key(seed), 10)
    features = normal_values(key_list[0], (BATCH, H, W, C), 1.0, 6.0, ((1, 4), (2, 2)))
    w_first = normal_values(key_list[1], (5, 5, C, C), (25 * C) ** -0.5, 0.078125, ((3, 4),))
    bias_first = normal_values(key_list[2], (C,), 0.5, 3.0, ((0, 4),), jnp.float32)
    w_second = heavy_noise(key_list[3], (5, 5, C, C), (25 * C) ** -0.5, 0.109375, ((2, 4),), (2, 3, 4, 2.0))
    bias_second = normal_values(key_list[4], (C,), 0.5, 3.0, (), jnp.float32)
    norm_gain = jnp.clip(1.0 + 0.15 * jax.random.normal(key_list[5], (C,), jnp.float32), 0.25, 1.75)
    norm_shift = normal_values(key_list[6], (C,), 0.5, 3.0, (), jnp.float32)
    w_down = normal_values(key_list[7], (2, 2, C, C), (4 * C) ** -0.5, 0.1875, ((3, 4),))
    bias_down = normal_values(key_list[8], (C,), 0.5, 3.0, ((0, 4),), jnp.float32)
    return {"features": features, "w_first": w_first, "bias_first": bias_first, "w_second": w_second, "bias_second": bias_second, "norm_gain": norm_gain, "norm_shift": norm_shift, "w_down": w_down, "bias_down": bias_down}


def convolve(inputs, kernel, dilation):
    return lax.conv_general_dilated(inputs.astype(jnp.float32), kernel.astype(jnp.float32), (1, 1), [(2 * dilation, 2 * dilation), (2 * dilation, 2 * dilation)], rhs_dilation=(dilation, dilation), dimension_numbers=('NHWC', 'HWIO', 'NHWC'), precision=lax.Precision.HIGHEST)

def reference(features, w_first, bias_first, w_second, bias_second, norm_gain, norm_shift, w_down, bias_down):
    hidden = jax.nn.gelu(convolve(features, w_first, 1) + bias_first).astype(jnp.bfloat16)
    group = C // N_CH
    summed = jnp.zeros(features.shape, jnp.float32)
    for index in range(N_CH):
        part = convolve(hidden[..., index * group:(index + 1) * group], w_second[:, :, index * group:(index + 1) * group, :], 2).astype(jnp.bfloat16)
        part = lax.optimization_barrier(part)
        summed = summed + part.astype(jnp.float32)
    mixed = features.astype(jnp.float32) + summed + bias_second
    total = lax.optimization_barrier(jnp.sum(mixed, axis=3, keepdims=True))
    square_total = lax.optimization_barrier(jnp.sum(mixed * mixed, axis=3, keepdims=True))
    mean = total / C
    variance = square_total / C - mean * mean
    normed = ((mixed - mean) * lax.rsqrt(variance + 1e-05) * norm_gain + norm_shift).astype(jnp.bfloat16)
    blocks = normed.astype(jnp.float32).reshape(BATCH, H // 2, 2, W // 2, 2, C)
    result = jnp.einsum('bhiwjc,ijcd->bhwd', blocks, w_down.astype(jnp.float32), precision=lax.Precision.HIGHEST)
    return (result + bias_down).astype(jnp.bfloat16)
```

```python
import functools

import jax
import jax.numpy as jnp
from jax import lax
from jax.experimental import pallas as pl
from jax.experimental.pallas import tpu as pltpu
from jax.sharding import PartitionSpec as P

MESH = pl.DeviceIdType.MESH
SIDE = 16
DIRECTIONS = ((0, -1), (0, 1), (-1, 0), (1, 0), (-1, -1), (-1, 1), (1, -1), (1, 1))


def span(step, halo, size, inner):
    if step == 0:
        return pl.ds(0, size), pl.ds(inner, size)
    if step < 0:
        return pl.ds(0, halo), pl.ds(inner + size, halo)
    return pl.ds(size - halo, halo), pl.ds(inner - halo, halo)


def kernel(
    counts,
    f_ref, w1_ref, b1_ref, w2_ref, b2_ref, gain_ref, shift_ref, wd_ref, bd_ref,
    out_ref,
    xp, hid, cols_ref, w1, w2, wd, bd, pb, got, nf, ob,
    local_sem, fs, fr, hs, hr, ws, wr, vs, vr, bs, br, ps, pr, os_, or_,
):
    n_lat, n_lon, n_ch = counts
    rows, cols, width = f_ref.shape
    share = w1_ref.shape[1] // 5
    per = rows // n_ch
    lat, lon, ch = lax.axis_index("lat"), lax.axis_index("lon"), lax.axis_index("ch")
    half = lax.rem(lon, 2)
    partner = lon + 1 - 2 * half

    loads = [
        pltpu.make_async_copy(f_ref, xp.at[pl.ds(2, rows), pl.ds(SIDE, cols)], local_sem.at[0]),
        pltpu.make_async_copy(w1_ref, w1, local_sem.at[1]),
        pltpu.make_async_copy(w2_ref, w2, local_sem.at[2]),
        pltpu.make_async_copy(wd_ref, wd.at[ch], local_sem.at[3]),
        pltpu.make_async_copy(bd_ref, bd.at[ch], local_sem.at[4]),
    ]
    for load in loads:
        load.start()

    def present(dy, dx):
        ok = None
        for step, at, count in ((dy, lat, n_lat), (dx, lon, n_lon)):
            if step:
                here = (at > 0) if step < 0 else (at < count - 1)
                ok = here if ok is None else jnp.logical_and(ok, here)
        return ok

    barrier = pltpu.get_barrier_semaphore()
    expected = jnp.int32(n_ch - 1)
    for dy, dx in DIRECTIONS:
        there = present(dy, dx)
        expected = expected + jnp.where(there, 1, 0)

        @pl.when(there)
        def _(dy=dy, dx=dx):
            pl.semaphore_signal(barrier, inc=1, device_id=(lat + dy, lon + dx, ch), device_id_type=MESH)

    peers = [lax.rem(ch + k, n_ch) for k in range(n_ch)]
    for k in range(1, n_ch):
        pl.semaphore_signal(barrier, inc=1, device_id=(lat, lon, peers[k]), device_id_type=MESH)
    pl.semaphore_wait(barrier, expected)

    def halo(index, source, pad, inner, height, send, recv):
        dy, dx = DIRECTIONS[index]
        from_y, to_y = span(dy, height, rows, height)
        from_x, to_x = span(dx, SIDE, cols, SIDE)
        if inner:
            from_y = pl.ds(from_y.start + height, from_y.size)
            from_x = pl.ds(from_x.start + SIDE, from_x.size)
        return pltpu.make_async_remote_copy(
            source.at[from_y, from_x], pad.at[to_y, to_x], send.at[index], recv.at[index],
            device_id=(lat + dy, lon + dx, ch), device_id_type=MESH,
        )

    def feature_halo(index):
        return halo(index, f_ref, xp, False, 2, fs, fr)

    def hidden_halo(index):
        return halo(index, hid, hid, True, 4, hs, hr)

    def start(copy_of, indices):
        for index in indices:
            @pl.when(present(*DIRECTIONS[index]))
            def _(index=index):
                copy_of(index).start()

    def arrive(copy_of, indices):
        for index in indices:
            dy, dx = DIRECTIONS[index]

            @pl.when(present(-dy, -dx))
            def _(index=index):
                copy_of(index).wait_recv()

    def drain(copy_of, indices):
        for index in indices:
            @pl.when(present(*DIRECTIONS[index]))
            def _(index=index):
                copy_of(index).wait_send()

    start(feature_halo, range(8))

    def weight_send(k):
        part = pl.ds(2 * half, 2)
        return pltpu.make_async_remote_copy(
            wd_ref.at[part], wd.at[ch, part], ws.at[k], wr.at[k],
            device_id=(lat, lon, peers[k]), device_id_type=MESH,
        )

    def bias_send(k):
        return pltpu.make_async_remote_copy(
            bd_ref, bd.at[ch], bs.at[k], br.at[k],
            device_id=(lat, lon, peers[k]), device_id_type=MESH,
        )

    def weight_pass(k, which):
        origin = lax.rem(ch + n_ch - k, n_ch)
        part = pl.ds(2 * which, 2)
        return pltpu.make_async_remote_copy(
            wd.at[origin, part], wd.at[origin, part], vs.at[k], vr.at[k],
            device_id=(lat, partner, ch), device_id_type=MESH,
        )

    for k in range(1, n_ch):
        weight_send(k).start()
        bias_send(k).start()

    for pad, height in ((xp, 2), (hid, 4)):
        @pl.when(lat == 0)
        def _():
            pad[0:height] = jnp.zeros((height,) + pad.shape[1:], pad.dtype)

        @pl.when(lat == n_lat - 1)
        def _():
            pad[rows + height :] = jnp.zeros((height,) + pad.shape[1:], pad.dtype)

        @pl.when(lon == 0)
        def _():
            pad[:, 0:SIDE] = jnp.zeros((rows + 2 * height, SIDE, pad.shape[2]), pad.dtype)

        @pl.when(lon == n_lon - 1)
        def _():
            pad[:, cols + SIDE :] = jnp.zeros((rows + 2 * height, SIDE, pad.shape[2]), pad.dtype)

    span_cols = cols + 2 * SIDE

    def first(begin, count):
        total = None
        for tap in range(5):
            window = xp[pl.ds(begin + tap, count)].reshape(count * span_cols, width)
            term = lax.dot_general(
                window, w1[tap], (((1,), (1,)), ((), ())), preferred_element_type=jnp.float32
            )
            total = term if total is None else total + term
        total = total.reshape(count, span_cols, 5 * share)
        value = None
        for tap in range(5):
            low = SIDE - 2 + tap
            piece = total[:, low : low + cols, tap * share : (tap + 1) * share]
            value = piece if value is None else value + piece
        value = jax.nn.gelu(value + b1_ref[...][None], approximate=True)
        hid[pl.ds(begin + 4, count), pl.ds(SIDE, cols)] = value.astype(jnp.bfloat16)

    loads[0].wait()
    loads[1].wait()
    arrive(feature_halo, range(2))

    @pl.loop(0, (rows - 4) // 4)
    def _(step):
        first(2 + 4 * step, 4)

    arrive(feature_halo, range(2, 8))
    first(0, 2)
    first(rows - 2, 2)
    start(hidden_halo, range(8))

    for k in range(1, n_ch):
        weight_send(k).wait_recv()
        weight_pass(k, half).start()

    def spread(begin, count):
        pieces = [
            hid[pl.ds(begin, count), pl.ds(SIDE - 4 + 2 * tap, cols)] for tap in range(5)
        ]
        cols_ref[pl.ds(begin, count)] = jnp.concatenate(pieces, axis=2)

    def share_copy(block):
        return pltpu.make_async_remote_copy(
            pb.at[block], got.at[ch], ps.at[block], pr.at[ch],
            device_id=(lat, lon, block), device_id_type=MESH,
        )

    def second(block):
        total = None
        for tap in range(5):
            window = cols_ref[pl.ds(per * block + 2 * tap, per)].reshape(per * cols, 5 * share)
            term = jnp.dot(window, w2[tap], preferred_element_type=jnp.float32)
            total = term if total is None else total + term
        pb[block] = total.astype(jnp.bfloat16).reshape(per, cols, width)

        @pl.when(ch != block)
        def _():
            share_copy(block).start()

    arrive(hidden_halo, range(2))
    loads[2].wait()

    @pl.loop(0, rows // 4)
    def _(step):
        spread(4 + 4 * step, 4)

    inner = [b for b in range(n_ch) if per * b >= 4 and per * (b + 1) + 4 <= rows]
    for block in inner:
        second(block)
    arrive(hidden_halo, range(2, 8))
    spread(0, 4)
    spread(rows + 4, 4)
    for block in range(n_ch):
        if block not in inner:
            second(block)

    mixed = xp[pl.ds(2 + per * ch, per), pl.ds(SIDE, cols)].astype(jnp.float32) + b2_ref[...][None]
    mixed = mixed + pb[ch].astype(jnp.float32)
    for k in range(1, n_ch):
        origin = peers[k]
        pltpu.make_async_remote_copy(
            pb.at[0], got.at[origin], ps.at[0], pr.at[origin],
            device_id=(lat, lon, origin), device_id_type=MESH,
        ).wait_recv()
        mixed = mixed + got[origin].astype(jnp.float32)
    mean = jnp.sum(mixed, axis=2, keepdims=True) / width
    variance = jnp.sum(mixed * mixed, axis=2, keepdims=True) / width - mean * mean
    normed = (mixed - mean) * lax.rsqrt(variance + 1e-05) * gain_ref[...][None] + shift_ref[...][None]
    normed = normed.astype(jnp.bfloat16).astype(jnp.float32).reshape(per * cols, width)
    for part in range(width // 128):
        nf[part] = normed[:, part * 128 : (part + 1) * 128]

    loads[3].wait()
    loads[4].wait()
    for k in range(1, n_ch):
        bias_send(k).wait_recv()
        weight_pass(k, 1 - half).wait_recv()

    result = None
    for tap in range(4):
        i, j = tap // 2, tap % 2
        picked = [
            jnp.concatenate(
                [
                    nf[part, pl.ds((2 * r + i) * cols + j, cols // 2, stride=2), :]
                    for part in range(width // 128)
                ],
                axis=1,
            )
            for r in range(per // 2)
        ]
        window = jnp.concatenate(picked, axis=0).astype(jnp.bfloat16)
        term = lax.dot_general(
            window, wd[:, tap].reshape(n_ch * share, width), (((1,), (1,)), ((), ())),
            preferred_element_type=jnp.float32,
        )
        result = term if result is None else result + term
    for to in range(n_ch):
        piece = result[:, to * share : (to + 1) * share] + bd[to]
        ob[to] = piece.astype(jnp.bfloat16).reshape(per // 2, cols // 2, share)

    def out_copy(k):
        place = pl.ds((per // 2) * ch, per // 2)
        return pltpu.make_async_remote_copy(
            ob.at[peers[k]], out_ref.at[place], os_.at[k], or_.at[k],
            device_id=(lat, lon, peers[k]), device_id_type=MESH,
        )

    own = pltpu.make_async_copy(ob.at[ch], out_ref.at[pl.ds((per // 2) * ch, per // 2)], local_sem.at[5])
    for k in range(1, n_ch):
        out_copy(k).start()
    own.start()

    drain(feature_halo, range(8))
    drain(hidden_halo, range(8))
    for k in range(1, n_ch):
        weight_send(k).wait_send()
        bias_send(k).wait_send()
        weight_pass(k, half).wait_send()
    for block in range(n_ch):
        @pl.when(ch != block)
        def _(block=block):
            share_copy(block).wait_send()
    own.wait()
    for k in range(1, n_ch):
        out_copy(k).wait_send()
        origin = lax.rem(ch + n_ch - k, n_ch)
        pltpu.make_async_remote_copy(
            ob.at[0], out_ref.at[pl.ds((per // 2) * origin, per // 2)], os_.at[k], or_.at[k],
            device_id=(lat, lon, peers[k]), device_id_type=MESH,
        ).wait_recv()


def body(counts, features, w_first, bias_first, w_second, bias_second, norm_gain, norm_shift, w_down, bias_down):
    _, rows, cols, width = features.shape
    n_ch = counts[2]
    share = w_first.shape[3]
    per = rows // n_ch
    bf16, f32 = jnp.bfloat16, jnp.float32
    dma = pltpu.SemaphoreType.DMA
    anywhere = pl.BlockSpec(memory_space=pl.ANY)
    vmem = pl.BlockSpec(memory_space=pltpu.VMEM)
    result = pl.pallas_call(
        functools.partial(kernel, counts),
        out_shape=jax.ShapeDtypeStruct((rows // 2, cols // 2, share), bf16),
        in_specs=[anywhere, anywhere, vmem, anywhere, vmem, vmem, vmem, anywhere, vmem],
        out_specs=anywhere,
        scratch_shapes=[
            pltpu.VMEM((rows + 4, cols + 2 * SIDE, width), bf16),
            pltpu.VMEM((rows + 8, cols + 2 * SIDE, share), bf16),
            pltpu.VMEM((rows + 8, cols, 5 * share), bf16),
            pltpu.VMEM((5, 5 * share, width), bf16),
            pltpu.VMEM((5, 5 * share, width), bf16),
            pltpu.VMEM((n_ch, 4, share, width), bf16),
            pltpu.VMEM((n_ch, 1, share), f32),
            pltpu.VMEM((n_ch, per, cols, width), bf16),
            pltpu.VMEM((n_ch, per, cols, width), bf16),
            pltpu.VMEM((width // 128, per * cols, 128), f32),
            pltpu.VMEM((n_ch, per // 2, cols // 2, share), bf16),
            dma((6,)), dma((8,)), dma((8,)), dma((8,)), dma((8,)),
            dma((n_ch,)), dma((n_ch,)), dma((n_ch,)), dma((n_ch,)), dma((n_ch,)), dma((n_ch,)),
            dma((n_ch,)), dma((n_ch,)), dma((n_ch,)), dma((n_ch,)),
        ],
        compiler_params=pltpu.CompilerParams(
            collective_id=0, has_side_effects=True, vmem_limit_bytes=40 * 1024 * 1024
        ),
        cost_estimate=pl.CostEstimate(flops=1700000000, bytes_accessed=3000000, transcendentals=70000),
    )(
        features[0],
        jnp.transpose(w_first, (0, 1, 3, 2)).reshape(5, 5 * share, width),
        bias_first.reshape(1, share),
        w_second.reshape(5, 5 * share, width),
        bias_second.reshape(1, width),
        norm_gain.reshape(1, width),
        norm_shift.reshape(1, width),
        jnp.transpose(w_down, (0, 1, 3, 2)).reshape(4, share, width),
        bias_down.reshape(1, share),
    )
    return result[None]


def solution(mesh):
    placed = (
        P(None, "lat", "lon", None),
        P(None, None, None, "ch"),
        P("ch"),
        P(None, None, "ch", None),
        P(),
        P(),
        P(),
        P(None, None, None, "ch"),
        P("ch"),
    )
    counts = tuple(mesh.shape[name] for name in ("lat", "lon", "ch"))
    return jax.shard_map(
        functools.partial(body, counts),
        mesh=mesh, in_specs=placed, out_specs=P(None, "lat", "lon", "ch"), check_vma=False,
    )
```

```python
import functools

import jax
import jax.numpy as jnp
from jax import lax
from jax.experimental import pallas as pl
from jax.experimental.pallas import tpu as pltpu
from jax.sharding import PartitionSpec as P

MESH = pl.DeviceIdType.MESH
SIDE = 16
DIRECTIONS = ((0, -1), (0, 1), (-1, 0), (1, 0), (-1, -1), (-1, 1), (1, -1), (1, 1))


def span(step, halo, size, inner):
    if step == 0:
        return pl.ds(0, size), pl.ds(inner, size)
    if step < 0:
        return pl.ds(0, halo), pl.ds(inner + size, halo)
    return pl.ds(size - halo, halo), pl.ds(inner - halo, halo)


def kernel(
    counts,
    f_ref, w1_ref, b1_ref, w2_ref, b2_ref, gain_ref, shift_ref, wd_ref, bd_ref,
    out_ref,
    xp, hid, cols_ref, w1, w2, wd, bd, pb, got, nf, ob,
    local_sem, fs, fr, hs, hr, ws, wr, vs, vr, bs, br, ps, pr, os_, or_,
):
    n_lat, n_lon, n_ch = counts
    rows, cols, width = f_ref.shape
    share = w1_ref.shape[1] // 5
    per = rows // n_ch
    lat, lon, ch = lax.axis_index("lat"), lax.axis_index("lon"), lax.axis_index("ch")
    half = lax.rem(lon, 2)
    partner = lon + 1 - 2 * half

    loads = [
        pltpu.make_async_copy(f_ref, xp.at[pl.ds(2, rows), pl.ds(SIDE, cols)], local_sem.at[0]),
        pltpu.make_async_copy(w1_ref, w1, local_sem.at[1]),
        pltpu.make_async_copy(w2_ref, w2, local_sem.at[2]),
        pltpu.make_async_copy(wd_ref, wd.at[ch], local_sem.at[3]),
        pltpu.make_async_copy(bd_ref, bd.at[ch], local_sem.at[4]),
    ]
    for load in loads:
        load.start()

    def present(dy, dx):
        ok = None
        for step, at, count in ((dy, lat, n_lat), (dx, lon, n_lon)):
            if step:
                here = (at > 0) if step < 0 else (at < count - 1)
                ok = here if ok is None else jnp.logical_and(ok, here)
        return ok

    barrier = pltpu.get_barrier_semaphore()
    expected = jnp.int32(n_ch - 1)
    for dy, dx in DIRECTIONS:
        there = present(dy, dx)
        expected = expected + jnp.where(there, 1, 0)

        @pl.when(there)
        def _(dy=dy, dx=dx):
            pl.semaphore_signal(barrier, inc=1, device_id=(lat + dy, lon + dx, ch), device_id_type=MESH)

    peers = [lax.rem(ch + k, n_ch) for k in range(n_ch)]
    for k in range(1, n_ch):
        pl.semaphore_signal(barrier, inc=1, device_id=(lat, lon, peers[k]), device_id_type=MESH)
    pl.semaphore_wait(barrier, expected)

    def halo(index, source, pad, inner, height, send, recv):
        dy, dx = DIRECTIONS[index]
        from_y, to_y = span(dy, height, rows, height)
        from_x, to_x = span(dx, SIDE, cols, SIDE)
        if inner:
            from_y = pl.ds(from_y.start + height, from_y.size)
            from_x = pl.ds(from_x.start + SIDE, from_x.size)
        return pltpu.make_async_remote_copy(
            source.at[from_y, from_x], pad.at[to_y, to_x], send.at[index], recv.at[index],
            device_id=(lat + dy, lon + dx, ch), device_id_type=MESH,
        )

    def feature_halo(index):
        return halo(index, f_ref, xp, False, 2, fs, fr)

    def hidden_halo(index):
        return halo(index, hid, hid, True, 4, hs, hr)

    def start(copy_of, indices):
        for index in indices:
            @pl.when(present(*DIRECTIONS[index]))
            def _(index=index):
                copy_of(index).start()

    def arrive(copy_of, indices):
        for index in indices:
            dy, dx = DIRECTIONS[index]

            @pl.when(present(-dy, -dx))
            def _(index=index):
                copy_of(index).wait_recv()

    def drain(copy_of, indices):
        for index in indices:
            @pl.when(present(*DIRECTIONS[index]))
            def _(index=index):
                copy_of(index).wait_send()

    start(feature_halo, range(8))

    def weight_send(k):
        part = pl.ds(2 * half, 2)
        return pltpu.make_async_remote_copy(
            wd_ref.at[part], wd.at[ch, part], ws.at[k], wr.at[k],
            device_id=(lat, lon, peers[k]), device_id_type=MESH,
        )

    def bias_send(k):
        return pltpu.make_async_remote_copy(
            bd_ref, bd.at[ch], bs.at[k], br.at[k],
            device_id=(lat, lon, peers[k]), device_id_type=MESH,
        )

    def weight_pass(k, which):
        origin = lax.rem(ch + n_ch - k, n_ch)
        part = pl.ds(2 * which, 2)
        return pltpu.make_async_remote_copy(
            wd.at[origin, part], wd.at[origin, part], vs.at[k], vr.at[k],
            device_id=(lat, partner, ch), device_id_type=MESH,
        )

    for k in range(1, n_ch):
        weight_send(k).start()
        bias_send(k).start()

    for pad, height in ((xp, 2), (hid, 4)):
        @pl.when(lat == 0)
        def _():
            pad[0:height] = jnp.zeros((height,) + pad.shape[1:], pad.dtype)

        @pl.when(lat == n_lat - 1)
        def _():
            pad[rows + height :] = jnp.zeros((height,) + pad.shape[1:], pad.dtype)

        @pl.when(lon == 0)
        def _():
            pad[:, 0:SIDE] = jnp.zeros((rows + 2 * height, SIDE, pad.shape[2]), pad.dtype)

        @pl.when(lon == n_lon - 1)
        def _():
            pad[:, cols + SIDE :] = jnp.zeros((rows + 2 * height, SIDE, pad.shape[2]), pad.dtype)

    span_cols = cols + 2 * SIDE

    def first(begin, count):
        total = None
        for tap in range(5):
            window = xp[pl.ds(begin + tap, count)].reshape(count * span_cols, width)
            term = lax.dot_general(
                window, w1[tap], (((1,), (1,)), ((), ())), preferred_element_type=jnp.float32
            )
            total = term if total is None else total + term
        total = total.reshape(count, span_cols, 5 * share)
        value = None
        for tap in range(5):
            low = SIDE - 2 + tap
            piece = total[:, low : low + cols, tap * share : (tap + 1) * share]
            value = piece if value is None else value + piece
        value = jax.nn.gelu(value + b1_ref[...][None], approximate=True)
        hid[pl.ds(begin + 4, count), pl.ds(SIDE, cols)] = value.astype(jnp.bfloat16)

    loads[0].wait()
    loads[1].wait()
    arrive(feature_halo, range(2))

    @pl.loop(0, (rows - 4) // 4)
    def _(step):
        first(2 + 4 * step, 4)

    arrive(feature_halo, range(2, 8))
    first(0, 2)
    first(rows - 2, 2)
    start(hidden_halo, range(8))

    for k in range(1, n_ch):
        weight_send(k).wait_recv()
        weight_pass(k, half).start()

    def spread(begin, count):
        pieces = [
            hid[pl.ds(begin, count), pl.ds(SIDE - 4 + 2 * tap, cols)] for tap in range(5)
        ]
        cols_ref[pl.ds(begin, count)] = jnp.concatenate(pieces, axis=2)

    def share_copy(block):
        return pltpu.make_async_remote_copy(
            pb.at[block], got.at[ch], ps.at[block], pr.at[ch],
            device_id=(lat, lon, block), device_id_type=MESH,
        )

    def second(block):
        total = None
        for tap in range(5):
            window = cols_ref[pl.ds(per * block + 2 * tap, per)].reshape(per * cols, 5 * share)
            term = jnp.dot(window, w2[tap], preferred_element_type=jnp.float32)
            total = term if total is None else total + term
        pb[block] = total.astype(jnp.bfloat16).reshape(per, cols, width)

        @pl.when(ch != block)
        def _():
            share_copy(block).start()

    arrive(hidden_halo, range(2))
    loads[2].wait()

    @pl.loop(0, rows // 4)
    def _(step):
        spread(4 + 4 * step, 4)

    inner = [b for b in range(n_ch) if per * b >= 4 and per * (b + 1) + 4 <= rows]
    for block in inner:
        second(block)
    arrive(hidden_halo, range(2, 8))
    spread(0, 4)
    spread(rows + 4, 4)
    for block in range(n_ch):
        if block not in inner:
            second(block)

    mixed = xp[pl.ds(2 + per * ch, per), pl.ds(SIDE, cols)].astype(jnp.float32) + b2_ref[...][None]
    mixed = mixed + pb[ch].astype(jnp.float32)
    for k in range(1, n_ch):
        origin = peers[k]
        pltpu.make_async_remote_copy(
            pb.at[0], got.at[origin], ps.at[0], pr.at[origin],
            device_id=(lat, lon, origin), device_id_type=MESH,
        ).wait_recv()
        mixed = mixed + got[origin].astype(jnp.float32)
    mean = jnp.sum(mixed, axis=2, keepdims=True) / width
    variance = jnp.sum(mixed * mixed, axis=2, keepdims=True) / width - mean * mean
    normed = (mixed - mean) * lax.rsqrt(variance + 1e-05) * gain_ref[...][None] + shift_ref[...][None]
    normed = normed.astype(jnp.bfloat16).astype(jnp.float32).reshape(per * cols, width)
    for part in range(width // 128):
        nf[part] = normed[:, part * 128 : (part + 1) * 128]

    loads[3].wait()
    loads[4].wait()
    for k in range(1, n_ch):
        bias_send(k).wait_recv()
        weight_pass(k, 1 - half).wait_recv()

    result = None
    for tap in range(4):
        i, j = tap // 2, tap % 2
        picked = [
            jnp.concatenate(
                [
                    nf[part, pl.ds((2 * r + i) * cols + j, cols // 2, stride=2), :]
                    for part in range(width // 128)
                ],
                axis=1,
            )
            for r in range(per // 2)
        ]
        window = jnp.concatenate(picked, axis=0).astype(jnp.bfloat16)
        term = lax.dot_general(
            window, wd[:, tap].reshape(n_ch * share, width), (((1,), (1,)), ((), ())),
            preferred_element_type=jnp.float32,
        )
        result = term if result is None else result + term
    for to in range(n_ch):
        piece = result[:, to * share : (to + 1) * share] + bd[to]
        ob[to] = piece.astype(jnp.bfloat16).reshape(per // 2, cols // 2, share)

    def out_copy(k):
        place = pl.ds((per // 2) * ch, per // 2)
        return pltpu.make_async_remote_copy(
            ob.at[peers[k]], out_ref.at[place], os_.at[k], or_.at[k],
            device_id=(lat, lon, peers[k]), device_id_type=MESH,
        )

    own = pltpu.make_async_copy(ob.at[ch], out_ref.at[pl.ds((per // 2) * ch, per // 2)], local_sem.at[5])
    for k in range(1, n_ch):
        out_copy(k).start()
    own.start()

    drain(feature_halo, range(8))
    drain(hidden_halo, range(8))
    for k in range(1, n_ch):
        weight_send(k).wait_send()
        bias_send(k).wait_send()
        weight_pass(k, half).wait_send()
    for block in range(n_ch):
        @pl.when(ch != block)
        def _(block=block):
            share_copy(block).wait_send()
    own.wait()
    for k in range(1, n_ch):
        out_copy(k).wait_send()
        origin = lax.rem(ch + n_ch - k, n_ch)
        pltpu.make_async_remote_copy(
            ob.at[0], out_ref.at[pl.ds((per // 2) * origin, per // 2)], os_.at[k], or_.at[k],
            device_id=(lat, lon, peers[k]), device_id_type=MESH,
        ).wait_recv()


def body(counts, features, w_first, bias_first, w_second, bias_second, norm_gain, norm_shift, w_down, bias_down):
    _, rows, cols, width = features.shape
    n_ch = counts[2]
    share = w_first.shape[3]
    per = rows // n_ch
    bf16, f32 = jnp.bfloat16, jnp.float32
    dma = pltpu.SemaphoreType.DMA
    anywhere = pl.BlockSpec(memory_space=pl.ANY)
    vmem = pl.BlockSpec(memory_space=pltpu.VMEM)
    result = pl.pallas_call(
        functools.partial(kernel, counts),
        out_shape=jax.ShapeDtypeStruct((rows // 2, cols // 2, share), bf16),
        in_specs=[anywhere, anywhere, vmem, anywhere, vmem, vmem, vmem, anywhere, vmem],
        out_specs=anywhere,
        scratch_shapes=[
            pltpu.VMEM((rows + 4, cols + 2 * SIDE, width), bf16),
            pltpu.VMEM((rows + 8, cols + 2 * SIDE, share), bf16),
            pltpu.VMEM((rows + 8, cols, 5 * share), bf16),
            pltpu.VMEM((5, 5 * share, width), bf16),
            pltpu.VMEM((5, 5 * share, width), bf16),
            pltpu.VMEM((n_ch, 4, share, width), bf16),
            pltpu.VMEM((n_ch, 1, share), f32),
            pltpu.VMEM((n_ch, per, cols, width), bf16),
            pltpu.VMEM((n_ch, per, cols, width), bf16),
            pltpu.VMEM((width // 128, per * cols, 128), f32),
            pltpu.VMEM((n_ch, per // 2, cols // 2, share), bf16),
            dma((6,)), dma((8,)), dma((8,)), dma((8,)), dma((8,)),
            dma((n_ch,)), dma((n_ch,)), dma((n_ch,)), dma((n_ch,)), dma((n_ch,)), dma((n_ch,)),
            dma((n_ch,)), dma((n_ch,)), dma((n_ch,)), dma((n_ch,)),
        ],
        compiler_params=pltpu.CompilerParams(
            collective_id=0, has_side_effects=True, vmem_limit_bytes=60 * 1024 * 1024
        ),
        cost_estimate=pl.CostEstimate(flops=1700000000, bytes_accessed=3000000, transcendentals=70000),
    )(
        features[0],
        jnp.transpose(w_first, (0, 1, 3, 2)).reshape(5, 5 * share, width),
        bias_first.reshape(1, share),
        w_second.reshape(5, 5 * share, width),
        bias_second.reshape(1, width),
        norm_gain.reshape(1, width),
        norm_shift.reshape(1, width),
        jnp.transpose(w_down, (0, 1, 3, 2)).reshape(4, share, width),
        bias_down.reshape(1, share),
    )
    return result[None]


def solution(mesh):
    placed = (
        P(None, "lat", "lon", None),
        P(None, None, None, "ch"),
        P("ch"),
        P(None, None, "ch", None),
        P(),
        P(),
        P(),
        P(None, None, None, "ch"),
        P("ch"),
    )
    counts = tuple(mesh.shape[name] for name in ("lat", "lon", "ch"))
    return jax.shard_map(
        functools.partial(body, counts),
        mesh=mesh, in_specs=placed, out_specs=P(None, "lat", "lon", "ch"), check_vma=False,
    )
```

```python
import functools

import jax
import jax.numpy as jnp
from jax import lax
from jax.experimental import pallas as pl
from jax.experimental.pallas import tpu as pltpu
from jax.sharding import PartitionSpec as P

MESH = pl.DeviceIdType.MESH
SIDE = 16
DIRECTIONS = ((0, -1), (0, 1), (-1, 0), (1, 0), (-1, -1), (-1, 1), (1, -1), (1, 1))


def span(step, halo, size, inner):
    if step == 0:
        return pl.ds(0, size), pl.ds(inner, size)
    if step < 0:
        return pl.ds(0, halo), pl.ds(inner + size, halo)
    return pl.ds(size - halo, halo), pl.ds(inner - halo, halo)


def kernel(
    counts,
    f_ref, w1_ref, b1_ref, w2_ref, b2_ref, gain_ref, shift_ref, wd_ref, bd_ref,
    out_ref,
    xp, hid, cols_ref, w1, w2, wd, bd, pb, got, nf, ob,
    local_sem, fs, fr, hs, hr, ws, wr, vs, vr, bs, br, ps, pr, os_, or_,
):
    n_lat, n_lon, n_ch = counts
    rows, cols, width = f_ref.shape
    share = w1_ref.shape[1] // 5
    per = rows // n_ch
    lat, lon, ch = lax.axis_index("lat"), lax.axis_index("lon"), lax.axis_index("ch")
    half = lax.rem(lon, 2)
    partner = lon + 1 - 2 * half

    loads = [
        pltpu.make_async_copy(f_ref, xp.at[pl.ds(2, rows), pl.ds(SIDE, cols)], local_sem.at[0]),
        pltpu.make_async_copy(w1_ref, w1, local_sem.at[1]),
        pltpu.make_async_copy(w2_ref, w2, local_sem.at[2]),
        pltpu.make_async_copy(wd_ref, wd.at[ch], local_sem.at[3]),
        pltpu.make_async_copy(bd_ref, bd.at[ch], local_sem.at[4]),
    ]
    for load in loads:
        load.start()

    def present(dy, dx):
        ok = None
        for step, at, count in ((dy, lat, n_lat), (dx, lon, n_lon)):
            if step:
                here = (at > 0) if step < 0 else (at < count - 1)
                ok = here if ok is None else jnp.logical_and(ok, here)
        return ok

    barrier = pltpu.get_barrier_semaphore()
    expected = jnp.int32(n_ch - 1)
    for dy, dx in DIRECTIONS:
        there = present(dy, dx)
        expected = expected + jnp.where(there, 1, 0)

        @pl.when(there)
        def _(dy=dy, dx=dx):
            pl.semaphore_signal(barrier, inc=1, device_id=(lat + dy, lon + dx, ch), device_id_type=MESH)

    peers = [lax.rem(ch + k, n_ch) for k in range(n_ch)]
    for k in range(1, n_ch):
        pl.semaphore_signal(barrier, inc=1, device_id=(lat, lon, peers[k]), device_id_type=MESH)
    pl.semaphore_wait(barrier, expected)

    def halo(index, source, pad, inner, height, send, recv):
        dy, dx = DIRECTIONS[index]
        from_y, to_y = span(dy, height, rows, height)
        from_x, to_x = span(dx, SIDE, cols, SIDE)
        if inner:
            from_y = pl.ds(from_y.start + height, from_y.size)
            from_x = pl.ds(from_x.start + SIDE, from_x.size)
        return pltpu.make_async_remote_copy(
            source.at[from_y, from_x], pad.at[to_y, to_x], send.at[index], recv.at[index],
            device_id=(lat + dy, lon + dx, ch), device_id_type=MESH,
        )

    def feature_halo(index):
        return halo(index, f_ref, xp, False, 2, fs, fr)

    def hidden_halo(index):
        return halo(index, hid, hid, True, 4, hs, hr)

    def start(copy_of, indices):
        for index in indices:
            @pl.when(present(*DIRECTIONS[index]))
            def _(index=index):
                copy_of(index).start()

    def arrive(copy_of, indices):
        for index in indices:
            dy, dx = DIRECTIONS[index]

            @pl.when(present(-dy, -dx))
            def _(index=index):
                copy_of(index).wait_recv()

    def drain(copy_of, indices):
        for index in indices:
            @pl.when(present(*DIRECTIONS[index]))
            def _(index=index):
                copy_of(index).wait_send()

    start(feature_halo, range(8))

    def weight_send(k):
        part = pl.ds(2 * half, 2)
        return pltpu.make_async_remote_copy(
            wd_ref.at[part], wd.at[ch, part], ws.at[k], wr.at[k],
            device_id=(lat, lon, peers[k]), device_id_type=MESH,
        )

    def bias_send(k):
        return pltpu.make_async_remote_copy(
            bd_ref, bd.at[ch], bs.at[k], br.at[k],
            device_id=(lat, lon, peers[k]), device_id_type=MESH,
        )

    def weight_pass(k, which):
        origin = lax.rem(ch + n_ch - k, n_ch)
        part = pl.ds(2 * which, 2)
        return pltpu.make_async_remote_copy(
            wd.at[origin, part], wd.at[origin, part], vs.at[k], vr.at[k],
            device_id=(lat, partner, ch), device_id_type=MESH,
        )

    for k in range(1, n_ch):
        weight_send(k).start()
        bias_send(k).start()

    for pad, height in ((xp, 2), (hid, 4)):
        @pl.when(lat == 0)
        def _():
            pad[0:height] = jnp.zeros((height,) + pad.shape[1:], pad.dtype)

        @pl.when(lat == n_lat - 1)
        def _():
            pad[rows + height :] = jnp.zeros((height,) + pad.shape[1:], pad.dtype)

        @pl.when(lon == 0)
        def _():
            pad[:, 0:SIDE] = jnp.zeros((rows + 2 * height, SIDE, pad.shape[2]), pad.dtype)

        @pl.when(lon == n_lon - 1)
        def _():
            pad[:, cols + SIDE :] = jnp.zeros((rows + 2 * height, SIDE, pad.shape[2]), pad.dtype)

    span_cols = cols + 2 * SIDE

    def first(begin, count):
        total = None
        for tap in range(5):
            window = xp[pl.ds(begin + tap, count)].reshape(count * span_cols, width)
            term = lax.dot_general(
                window, w1[tap], (((1,), (1,)), ((), ())), preferred_element_type=jnp.float32
            )
            total = term if total is None else total + term
        total = total.reshape(count, span_cols, 5 * share)
        value = None
        for tap in range(5):
            low = SIDE - 2 + tap
            piece = total[:, low : low + cols, tap * share : (tap + 1) * share]
            value = piece if value is None else value + piece
        value = jax.nn.gelu(value + b1_ref[...][None], approximate=True)
        hid[pl.ds(begin + 4, count), pl.ds(SIDE, cols)] = value.astype(jnp.bfloat16)

    loads[0].wait()
    loads[1].wait()
    arrive(feature_halo, range(2))

    @pl.loop(0, (rows - 4) // 4)
    def _(step):
        first(2 + 4 * step, 4)

    arrive(feature_halo, range(2, 8))
    first(0, 2)
    first(rows - 2, 2)
    start(hidden_halo, range(8))

    for k in range(1, n_ch):
        weight_send(k).wait_recv()
        weight_pass(k, half).start()

    def spread(begin, count):
        pieces = [
            hid[pl.ds(begin, count), pl.ds(SIDE - 4 + 2 * tap, cols)] for tap in range(5)
        ]
        cols_ref[pl.ds(begin, count)] = jnp.concatenate(pieces, axis=2)

    def share_copy(block):
        return pltpu.make_async_remote_copy(
            pb.at[block], got.at[ch], ps.at[block], pr.at[ch],
            device_id=(lat, lon, block), device_id_type=MESH,
        )

    def second(block, send):
        total = None
        for tap in range(5):
            window = cols_ref[pl.ds(per * block + 2 * tap, per)].reshape(per * cols, 5 * share)
            term = jnp.dot(window, w2[tap], preferred_element_type=jnp.float32)
            total = term if total is None else total + term
        pb[block] = total.astype(jnp.bfloat16).reshape(per, cols, width)
        if send:
            share_copy(block).start()

    arrive(hidden_halo, range(2))
    loads[2].wait()

    @pl.loop(0, rows // 4)
    def _(step):
        spread(4 + 4 * step, 4)

    middle = n_ch // 2
    low = ch < middle
    across = jnp.where(low, middle, middle - 1)
    outer = jnp.where(low, n_ch - 1, 0)
    beside = jnp.where(low, middle - 1 - ch, n_ch + middle - 1 - ch)
    second(across, True)
    arrive(hidden_halo, range(2, 8))
    spread(0, 4)
    spread(rows + 4, 4)
    second(outer, True)
    second(beside, True)
    second(ch, False)

    mixed = xp[pl.ds(2 + per * ch, per), pl.ds(SIDE, cols)].astype(jnp.float32) + b2_ref[...][None]
    mixed = mixed + pb[ch].astype(jnp.float32)
    for k in range(1, n_ch):
        origin = peers[k]
        pltpu.make_async_remote_copy(
            pb.at[0], got.at[origin], ps.at[0], pr.at[origin],
            device_id=(lat, lon, origin), device_id_type=MESH,
        ).wait_recv()
        mixed = mixed + got[origin].astype(jnp.float32)
    mean = jnp.sum(mixed, axis=2, keepdims=True) / width
    variance = jnp.sum(mixed * mixed, axis=2, keepdims=True) / width - mean * mean
    normed = (mixed - mean) * lax.rsqrt(variance + 1e-05) * gain_ref[...][None] + shift_ref[...][None]
    normed = normed.astype(jnp.bfloat16).astype(jnp.float32).reshape(per * cols, width)
    for part in range(width // 128):
        nf[part] = normed[:, part * 128 : (part + 1) * 128]

    loads[3].wait()
    loads[4].wait()
    for k in range(1, n_ch):
        bias_send(k).wait_recv()
        weight_pass(k, 1 - half).wait_recv()

    result = None
    for tap in range(4):
        i, j = tap // 2, tap % 2
        picked = [
            jnp.concatenate(
                [
                    nf[part, pl.ds((2 * r + i) * cols + j, cols // 2, stride=2), :]
                    for part in range(width // 128)
                ],
                axis=1,
            )
            for r in range(per // 2)
        ]
        window = jnp.concatenate(picked, axis=0).astype(jnp.bfloat16)
        term = lax.dot_general(
            window, wd[:, tap].reshape(n_ch * share, width), (((1,), (1,)), ((), ())),
            preferred_element_type=jnp.float32,
        )
        result = term if result is None else result + term
    for to in range(n_ch):
        piece = result[:, to * share : (to + 1) * share] + bd[to]
        ob[to] = piece.astype(jnp.bfloat16).reshape(per // 2, cols // 2, share)

    def out_copy(k):
        place = pl.ds((per // 2) * ch, per // 2)
        return pltpu.make_async_remote_copy(
            ob.at[peers[k]], out_ref.at[place], os_.at[k], or_.at[k],
            device_id=(lat, lon, peers[k]), device_id_type=MESH,
        )

    own = pltpu.make_async_copy(ob.at[ch], out_ref.at[pl.ds((per // 2) * ch, per // 2)], local_sem.at[5])
    for k in range(1, n_ch):
        out_copy(k).start()
    own.start()

    drain(feature_halo, range(8))
    drain(hidden_halo, range(8))
    for k in range(1, n_ch):
        weight_send(k).wait_send()
        bias_send(k).wait_send()
        weight_pass(k, half).wait_send()
    for block in (across, outer, beside):
        share_copy(block).wait_send()
    own.wait()
    for k in range(1, n_ch):
        out_copy(k).wait_send()
        origin = lax.rem(ch + n_ch - k, n_ch)
        pltpu.make_async_remote_copy(
            ob.at[0], out_ref.at[pl.ds((per // 2) * origin, per // 2)], os_.at[k], or_.at[k],
            device_id=(lat, lon, peers[k]), device_id_type=MESH,
        ).wait_recv()


def body(counts, features, w_first, bias_first, w_second, bias_second, norm_gain, norm_shift, w_down, bias_down):
    _, rows, cols, width = features.shape
    n_ch = counts[2]
    share = w_first.shape[3]
    per = rows // n_ch
    bf16, f32 = jnp.bfloat16, jnp.float32
    dma = pltpu.SemaphoreType.DMA
    anywhere = pl.BlockSpec(memory_space=pl.ANY)
    vmem = pl.BlockSpec(memory_space=pltpu.VMEM)
    result = pl.pallas_call(
        functools.partial(kernel, counts),
        out_shape=jax.ShapeDtypeStruct((rows // 2, cols // 2, share), bf16),
        in_specs=[anywhere, anywhere, vmem, anywhere, vmem, vmem, vmem, anywhere, vmem],
        out_specs=anywhere,
        scratch_shapes=[
            pltpu.VMEM((rows + 4, cols + 2 * SIDE, width), bf16),
            pltpu.VMEM((rows + 8, cols + 2 * SIDE, share), bf16),
            pltpu.VMEM((rows + 8, cols, 5 * share), bf16),
            pltpu.VMEM((5, 5 * share, width), bf16),
            pltpu.VMEM((5, 5 * share, width), bf16),
            pltpu.VMEM((n_ch, 4, share, width), bf16),
            pltpu.VMEM((n_ch, 1, share), f32),
            pltpu.VMEM((n_ch, per, cols, width), bf16),
            pltpu.VMEM((n_ch, per, cols, width), bf16),
            pltpu.VMEM((width // 128, per * cols, 128), f32),
            pltpu.VMEM((n_ch, per // 2, cols // 2, share), bf16),
            dma((6,)), dma((8,)), dma((8,)), dma((8,)), dma((8,)),
            dma((n_ch,)), dma((n_ch,)), dma((n_ch,)), dma((n_ch,)), dma((n_ch,)), dma((n_ch,)),
            dma((n_ch,)), dma((n_ch,)), dma((n_ch,)), dma((n_ch,)),
        ],
        compiler_params=pltpu.CompilerParams(
            collective_id=0, has_side_effects=True, vmem_limit_bytes=60 * 1024 * 1024
        ),
        cost_estimate=pl.CostEstimate(flops=1700000000, bytes_accessed=3000000, transcendentals=70000),
    )(
        features[0],
        jnp.transpose(w_first, (0, 1, 3, 2)).reshape(5, 5 * share, width),
        bias_first.reshape(1, share),
        w_second.reshape(5, 5 * share, width),
        bias_second.reshape(1, width),
        norm_gain.reshape(1, width),
        norm_shift.reshape(1, width),
        jnp.transpose(w_down, (0, 1, 3, 2)).reshape(4, share, width),
        bias_down.reshape(1, share),
    )
    return result[None]


def solution(mesh):
    placed = (
        P(None, "lat", "lon", None),
        P(None, None, None, "ch"),
        P("ch"),
        P(None, None, "ch", None),
        P(),
        P(),
        P(),
        P(None, None, None, "ch"),
        P("ch"),
    )
    counts = tuple(mesh.shape[name] for name in ("lat", "lon", "ch"))
    return jax.shard_map(
        functools.partial(body, counts),
        mesh=mesh, in_specs=placed, out_specs=P(None, "lat", "lon", "ch"), check_vma=False,
    )
```

```python
import functools

import jax
import jax.numpy as jnp
from jax import lax
from jax.experimental import pallas as pl
from jax.experimental.pallas import tpu as pltpu
from jax.sharding import PartitionSpec as P

MESH = pl.DeviceIdType.MESH
SIDE = 16
DIRECTIONS = ((0, -1), (0, 1), (-1, 0), (1, 0), (-1, -1), (-1, 1), (1, -1), (1, 1))


def span(step, halo, size, inner):
    if step == 0:
        return pl.ds(0, size), pl.ds(inner, size)
    if step < 0:
        return pl.ds(0, halo), pl.ds(inner + size, halo)
    return pl.ds(size - halo, halo), pl.ds(inner - halo, halo)


def kernel(
    counts,
    f_ref, w1_ref, b1_ref, w2_ref, b2_ref, gain_ref, shift_ref, wd_ref, bd_ref,
    out_ref,
    xp, hid, cols_ref, w1, w2, wd, bd, pb, got, via, nf, ob,
    local_sem, fs, fr, hs, hr, ws, wr, vs, vr, bs, br, ps, pr, rs, rr, os_, or_,
):
    n_lat, n_lon, n_ch = counts
    rows, cols, width = f_ref.shape
    share = w1_ref.shape[1] // 5
    per = rows // n_ch
    lat, lon, ch = lax.axis_index("lat"), lax.axis_index("lon"), lax.axis_index("ch")
    half = lax.rem(lon, 2)
    partner = lon + 1 - 2 * half

    loads = [
        pltpu.make_async_copy(f_ref, xp.at[pl.ds(2, rows), pl.ds(SIDE, cols)], local_sem.at[0]),
        pltpu.make_async_copy(w1_ref, w1, local_sem.at[1]),
        pltpu.make_async_copy(w2_ref, w2, local_sem.at[2]),
        pltpu.make_async_copy(wd_ref, wd.at[ch], local_sem.at[3]),
        pltpu.make_async_copy(bd_ref, bd.at[ch], local_sem.at[4]),
    ]
    for load in loads:
        load.start()

    def present(dy, dx):
        ok = None
        for step, at, count in ((dy, lat, n_lat), (dx, lon, n_lon)):
            if step:
                here = (at > 0) if step < 0 else (at < count - 1)
                ok = here if ok is None else jnp.logical_and(ok, here)
        return ok

    barrier = pltpu.get_barrier_semaphore()
    expected = jnp.int32(n_ch - 1)
    for dy, dx in DIRECTIONS:
        there = present(dy, dx)
        expected = expected + jnp.where(there, 1, 0)

        @pl.when(there)
        def _(dy=dy, dx=dx):
            pl.semaphore_signal(barrier, inc=1, device_id=(lat + dy, lon + dx, ch), device_id_type=MESH)

    peers = [lax.rem(ch + k, n_ch) for k in range(n_ch)]
    for k in range(1, n_ch):
        pl.semaphore_signal(barrier, inc=1, device_id=(lat, lon, peers[k]), device_id_type=MESH)
    pl.semaphore_wait(barrier, expected)

    def halo(index, source, pad, inner, height, send, recv):
        dy, dx = DIRECTIONS[index]
        from_y, to_y = span(dy, height, rows, height)
        from_x, to_x = span(dx, SIDE, cols, SIDE)
        if inner:
            from_y = pl.ds(from_y.start + height, from_y.size)
            from_x = pl.ds(from_x.start + SIDE, from_x.size)
        return pltpu.make_async_remote_copy(
            source.at[from_y, from_x], pad.at[to_y, to_x], send.at[index], recv.at[index],
            device_id=(lat + dy, lon + dx, ch), device_id_type=MESH,
        )

    def feature_halo(index):
        return halo(index, f_ref, xp, False, 2, fs, fr)

    def hidden_halo(index):
        return halo(index, hid, hid, True, 4, hs, hr)

    def start(copy_of, indices):
        for index in indices:
            @pl.when(present(*DIRECTIONS[index]))
            def _(index=index):
                copy_of(index).start()

    def arrive(copy_of, indices):
        for index in indices:
            dy, dx = DIRECTIONS[index]

            @pl.when(present(-dy, -dx))
            def _(index=index):
                copy_of(index).wait_recv()

    def drain(copy_of, indices):
        for index in indices:
            @pl.when(present(*DIRECTIONS[index]))
            def _(index=index):
                copy_of(index).wait_send()

    start(feature_halo, range(8))

    def weight_send(k):
        part = pl.ds(2 * half, 2)
        return pltpu.make_async_remote_copy(
            wd_ref.at[part], wd.at[ch, part], ws.at[k], wr.at[k],
            device_id=(lat, lon, peers[k]), device_id_type=MESH,
        )

    def bias_send(k):
        return pltpu.make_async_remote_copy(
            bd_ref, bd.at[ch], bs.at[k], br.at[k],
            device_id=(lat, lon, peers[k]), device_id_type=MESH,
        )

    def weight_pass(k, which):
        origin = lax.rem(ch + n_ch - k, n_ch)
        part = pl.ds(2 * which, 2)
        return pltpu.make_async_remote_copy(
            wd.at[origin, part], wd.at[origin, part], vs.at[k], vr.at[k],
            device_id=(lat, partner, ch), device_id_type=MESH,
        )

    for k in range(1, n_ch):
        weight_send(k).start()
        bias_send(k).start()

    for pad, height in ((xp, 2), (hid, 4)):
        @pl.when(lat == 0)
        def _():
            pad[0:height] = jnp.zeros((height,) + pad.shape[1:], pad.dtype)

        @pl.when(lat == n_lat - 1)
        def _():
            pad[rows + height :] = jnp.zeros((height,) + pad.shape[1:], pad.dtype)

        @pl.when(lon == 0)
        def _():
            pad[:, 0:SIDE] = jnp.zeros((rows + 2 * height, SIDE, pad.shape[2]), pad.dtype)

        @pl.when(lon == n_lon - 1)
        def _():
            pad[:, cols + SIDE :] = jnp.zeros((rows + 2 * height, SIDE, pad.shape[2]), pad.dtype)

    span_cols = cols + 2 * SIDE

    def first(begin, count):
        total = None
        for tap in range(5):
            window = xp[pl.ds(begin + tap, count)].reshape(count * span_cols, width)
            term = lax.dot_general(
                window, w1[tap], (((1,), (1,)), ((), ())), preferred_element_type=jnp.float32
            )
            total = term if total is None else total + term
        total = total.reshape(count, span_cols, 5 * share)
        value = None
        for tap in range(5):
            low = SIDE - 2 + tap
            piece = total[:, low : low + cols, tap * share : (tap + 1) * share]
            value = piece if value is None else value + piece
        value = jax.nn.gelu(value + b1_ref[...][None], approximate=True)
        hid[pl.ds(begin + 4, count), pl.ds(SIDE, cols)] = value.astype(jnp.bfloat16)

    loads[0].wait()
    loads[1].wait()
    arrive(feature_halo, range(2))

    @pl.loop(0, (rows - 4) // 4)
    def _(step):
        first(2 + 4 * step, 4)

    arrive(feature_halo, range(2, 8))
    first(0, 2)
    first(rows - 2, 2)
    start(hidden_halo, range(8))

    for k in range(1, n_ch):
        weight_send(k).wait_recv()
        weight_pass(k, half).start()

    def spread(begin, count):
        pieces = [
            hid[pl.ds(begin, count), pl.ds(SIDE - 4 + 2 * tap, cols)] for tap in range(5)
        ]
        cols_ref[pl.ds(begin, count)] = jnp.concatenate(pieces, axis=2)

    def second(block):
        total = None
        for tap in range(5):
            window = cols_ref[pl.ds(per * block + 2 * tap, per)].reshape(per * cols, 5 * share)
            term = jnp.dot(window, w2[tap], preferred_element_type=jnp.float32)
            total = term if total is None else total + term
        pb[block] = total.astype(jnp.bfloat16).reshape(per, cols, width)

    arrive(hidden_halo, range(2))
    loads[2].wait()

    @pl.loop(0, rows // 4)
    def _(step):
        spread(4 + 4 * step, 4)

    middle = n_ch // 2
    low = ch < middle
    across = jnp.where(low, middle, middle - 1)
    outer = jnp.where(low, n_ch - 1, 0)
    beside = jnp.where(low, middle - 1 - ch, n_ch + middle - 1 - ch)
    edge = jnp.logical_or(ch == 0, ch == n_ch - 1)
    inside = jnp.logical_not(edge)
    far = (across, outer)

    def relay_copy(n):
        return pltpu.make_async_remote_copy(
            pb.at[far[n]], via.at[n], rs.at[n], rr.at[n],
            device_id=(lat, lon, beside), device_id_type=MESH,
        )

    def share_copy(n, block):
        return pltpu.make_async_remote_copy(
            pb.at[block], got.at[ch], ps.at[n], pr.at[ch],
            device_id=(lat, lon, block), device_id_type=MESH,
        )

    second(across)

    @pl.when(edge)
    def _():
        relay_copy(0).start()

    arrive(hidden_halo, range(2, 8))
    spread(0, 4)
    spread(rows + 4, 4)
    second(outer)

    @pl.when(edge)
    def _():
        relay_copy(1).start()

    second(beside)
    share_copy(2, beside).start()

    @pl.when(inside)
    def _():
        for n in range(2):
            relay_copy(n).wait_recv()
            both = pb[far[n]].astype(jnp.float32) + via[n].astype(jnp.float32)
            pb[far[n]] = both.astype(jnp.bfloat16)
            share_copy(n, far[n]).start()

    second(ch)

    mixed = xp[pl.ds(2 + per * ch, per), pl.ds(SIDE, cols)].astype(jnp.float32) + b2_ref[...][None]
    mixed = mixed + pb[ch].astype(jnp.float32)
    for origin in (beside, across):
        pltpu.make_async_remote_copy(
            pb.at[0], got.at[origin], ps.at[0], pr.at[origin],
            device_id=(lat, lon, origin), device_id_type=MESH,
        ).wait_recv()
        mixed = mixed + got[origin].astype(jnp.float32)
    mean = jnp.sum(mixed, axis=2, keepdims=True) / width
    variance = jnp.sum(mixed * mixed, axis=2, keepdims=True) / width - mean * mean
    normed = (mixed - mean) * lax.rsqrt(variance + 1e-05) * gain_ref[...][None] + shift_ref[...][None]
    normed = normed.astype(jnp.bfloat16).astype(jnp.float32).reshape(per * cols, width)
    for part in range(width // 128):
        nf[part] = normed[:, part * 128 : (part + 1) * 128]

    loads[3].wait()
    loads[4].wait()
    for k in range(1, n_ch):
        bias_send(k).wait_recv()
        weight_pass(k, 1 - half).wait_recv()

    result = None
    for tap in range(4):
        i, j = tap // 2, tap % 2
        picked = [
            jnp.concatenate(
                [
                    nf[part, pl.ds((2 * r + i) * cols + j, cols // 2, stride=2), :]
                    for part in range(width // 128)
                ],
                axis=1,
            )
            for r in range(per // 2)
        ]
        window = jnp.concatenate(picked, axis=0).astype(jnp.bfloat16)
        term = lax.dot_general(
            window, wd[:, tap].reshape(n_ch * share, width), (((1,), (1,)), ((), ())),
            preferred_element_type=jnp.float32,
        )
        result = term if result is None else result + term
    for to in range(n_ch):
        piece = result[:, to * share : (to + 1) * share] + bd[to]
        ob[to] = piece.astype(jnp.bfloat16).reshape(per // 2, cols // 2, share)

    def out_copy(k):
        place = pl.ds((per // 2) * ch, per // 2)
        return pltpu.make_async_remote_copy(
            ob.at[peers[k]], out_ref.at[place], os_.at[k], or_.at[k],
            device_id=(lat, lon, peers[k]), device_id_type=MESH,
        )

    own = pltpu.make_async_copy(ob.at[ch], out_ref.at[pl.ds((per // 2) * ch, per // 2)], local_sem.at[5])
    for k in range(1, n_ch):
        out_copy(k).start()
    own.start()

    drain(feature_halo, range(8))
    drain(hidden_halo, range(8))
    for k in range(1, n_ch):
        weight_send(k).wait_send()
        bias_send(k).wait_send()
        weight_pass(k, half).wait_send()
    share_copy(2, beside).wait_send()
    for n in range(2):
        @pl.when(edge)
        def _(n=n):
            relay_copy(n).wait_send()

        @pl.when(inside)
        def _(n=n):
            share_copy(n, far[n]).wait_send()
    own.wait()
    for k in range(1, n_ch):
        out_copy(k).wait_send()
        origin = lax.rem(ch + n_ch - k, n_ch)
        pltpu.make_async_remote_copy(
            ob.at[0], out_ref.at[pl.ds((per // 2) * origin, per // 2)], os_.at[k], or_.at[k],
            device_id=(lat, lon, peers[k]), device_id_type=MESH,
        ).wait_recv()


def body(counts, features, w_first, bias_first, w_second, bias_second, norm_gain, norm_shift, w_down, bias_down):
    _, rows, cols, width = features.shape
    n_ch = counts[2]
    share = w_first.shape[3]
    per = rows // n_ch
    bf16, f32 = jnp.bfloat16, jnp.float32
    dma = pltpu.SemaphoreType.DMA
    anywhere = pl.BlockSpec(memory_space=pl.ANY)
    vmem = pl.BlockSpec(memory_space=pltpu.VMEM)
    result = pl.pallas_call(
        functools.partial(kernel, counts),
        out_shape=jax.ShapeDtypeStruct((rows // 2, cols // 2, share), bf16),
        in_specs=[anywhere, anywhere, vmem, anywhere, vmem, vmem, vmem, anywhere, vmem],
        out_specs=anywhere,
        scratch_shapes=[
            pltpu.VMEM((rows + 4, cols + 2 * SIDE, width), bf16),
            pltpu.VMEM((rows + 8, cols + 2 * SIDE, share), bf16),
            pltpu.VMEM((rows + 8, cols, 5 * share), bf16),
            pltpu.VMEM((5, 5 * share, width), bf16),
            pltpu.VMEM((5, 5 * share, width), bf16),
            pltpu.VMEM((n_ch, 4, share, width), bf16),
            pltpu.VMEM((n_ch, 1, share), f32),
            pltpu.VMEM((n_ch, per, cols, width), bf16),
            pltpu.VMEM((n_ch, per, cols, width), bf16),
            pltpu.VMEM((2, per, cols, width), bf16),
            pltpu.VMEM((width // 128, per * cols, 128), f32),
            pltpu.VMEM((n_ch, per // 2, cols // 2, share), bf16),
            dma((6,)), dma((8,)), dma((8,)), dma((8,)), dma((8,)),
            dma((n_ch,)), dma((n_ch,)), dma((n_ch,)), dma((n_ch,)), dma((n_ch,)), dma((n_ch,)),
            dma((n_ch,)), dma((n_ch,)), dma((2,)), dma((2,)), dma((n_ch,)), dma((n_ch,)),
        ],
        compiler_params=pltpu.CompilerParams(
            collective_id=0, has_side_effects=True, vmem_limit_bytes=60 * 1024 * 1024
        ),
        cost_estimate=pl.CostEstimate(flops=1700000000, bytes_accessed=3000000, transcendentals=70000),
    )(
        features[0],
        jnp.transpose(w_first, (0, 1, 3, 2)).reshape(5, 5 * share, width),
        bias_first.reshape(1, share),
        w_second.reshape(5, 5 * share, width),
        bias_second.reshape(1, width),
        norm_gain.reshape(1, width),
        norm_shift.reshape(1, width),
        jnp.transpose(w_down, (0, 1, 3, 2)).reshape(4, share, width),
        bias_down.reshape(1, share),
    )
    return result[None]


def solution(mesh):
    placed = (
        P(None, "lat", "lon", None),
        P(None, None, None, "ch"),
        P("ch"),
        P(None, None, "ch", None),
        P(),
        P(),
        P(),
        P(None, None, None, "ch"),
        P("ch"),
    )
    counts = tuple(mesh.shape[name] for name in ("lat", "lon", "ch"))
    return jax.shard_map(
        functools.partial(body, counts),
        mesh=mesh, in_specs=placed, out_specs=P(None, "lat", "lon", "ch"), check_vma=False,
    )
```

```python
import functools

import jax
import jax.numpy as jnp
from jax import lax
from jax.experimental import pallas as pl
from jax.experimental.pallas import tpu as pltpu
from jax.sharding import PartitionSpec as P

MESH = pl.DeviceIdType.MESH
SIDE = 16
DIRECTIONS = ((0, -1), (0, 1), (-1, 0), (1, 0), (-1, -1), (-1, 1), (1, -1), (1, 1))


def span(step, halo, size, inner):
    if step == 0:
        return pl.ds(0, size), pl.ds(inner, size)
    if step < 0:
        return pl.ds(0, halo), pl.ds(inner + size, halo)
    return pl.ds(size - halo, halo), pl.ds(inner - halo, halo)


def kernel(
    counts,
    f_ref, w1_ref, b1_ref, w2_ref, b2_ref, gain_ref, shift_ref, wd_ref, bd_ref,
    out_ref,
    xp, hid, cols_ref, w1, w2, wd, bd, pb, got, via, nf, ob,
    local_sem, fs, fr, hs, hr, ws, wr, vs, vr, bs, br, ps, pr, rs, rr, os_, or_,
):
    n_lat, n_lon, n_ch = counts
    rows, cols, width = f_ref.shape
    share = w1_ref.shape[1] // 5
    per = rows // n_ch
    lat, lon, ch = lax.axis_index("lat"), lax.axis_index("lon"), lax.axis_index("ch")
    half = lax.rem(lon, 2)
    partner = lon + 1 - 2 * half

    loads = [
        pltpu.make_async_copy(f_ref, xp.at[pl.ds(2, rows), pl.ds(SIDE, cols)], local_sem.at[0]),
        pltpu.make_async_copy(w1_ref, w1, local_sem.at[1]),
        pltpu.make_async_copy(w2_ref, w2, local_sem.at[2]),
        pltpu.make_async_copy(wd_ref, wd.at[ch], local_sem.at[3]),
        pltpu.make_async_copy(bd_ref, bd.at[ch], local_sem.at[4]),
    ]
    for load in loads:
        load.start()

    def present(dy, dx):
        ok = None
        for step, at, count in ((dy, lat, n_lat), (dx, lon, n_lon)):
            if step:
                here = (at > 0) if step < 0 else (at < count - 1)
                ok = here if ok is None else jnp.logical_and(ok, here)
        return ok

    barrier = pltpu.get_barrier_semaphore()
    expected = jnp.int32(n_ch - 1)
    for dy, dx in DIRECTIONS:
        there = present(dy, dx)
        expected = expected + jnp.where(there, 1, 0)

        @pl.when(there)
        def _(dy=dy, dx=dx):
            pl.semaphore_signal(barrier, inc=1, device_id=(lat + dy, lon + dx, ch), device_id_type=MESH)

    peers = [lax.rem(ch + k, n_ch) for k in range(n_ch)]
    for k in range(1, n_ch):
        pl.semaphore_signal(barrier, inc=1, device_id=(lat, lon, peers[k]), device_id_type=MESH)
    pl.semaphore_wait(barrier, expected)

    def halo(index, source, pad, inner, height, send, recv):
        dy, dx = DIRECTIONS[index]
        from_y, to_y = span(dy, height, rows, height)
        from_x, to_x = span(dx, SIDE, cols, SIDE)
        if inner:
            from_y = pl.ds(from_y.start + height, from_y.size)
            from_x = pl.ds(from_x.start + SIDE, from_x.size)
        return pltpu.make_async_remote_copy(
            source.at[from_y, from_x], pad.at[to_y, to_x], send.at[index], recv.at[index],
            device_id=(lat + dy, lon + dx, ch), device_id_type=MESH,
        )

    def feature_halo(index):
        return halo(index, f_ref, xp, False, 2, fs, fr)

    def hidden_halo(index):
        return halo(index, hid, hid, True, 4, hs, hr)

    def start(copy_of, indices):
        for index in indices:
            @pl.when(present(*DIRECTIONS[index]))
            def _(index=index):
                copy_of(index).start()

    def arrive(copy_of, indices):
        for index in indices:
            dy, dx = DIRECTIONS[index]

            @pl.when(present(-dy, -dx))
            def _(index=index):
                copy_of(index).wait_recv()

    def drain(copy_of, indices):
        for index in indices:
            @pl.when(present(*DIRECTIONS[index]))
            def _(index=index):
                copy_of(index).wait_send()

    start(feature_halo, range(8))

    def weight_send(k):
        part = pl.ds(2 * half, 2)
        return pltpu.make_async_remote_copy(
            wd_ref.at[part], wd.at[ch, part], ws.at[k], wr.at[k],
            device_id=(lat, lon, peers[k]), device_id_type=MESH,
        )

    def bias_send(k):
        return pltpu.make_async_remote_copy(
            bd_ref, bd.at[ch], bs.at[k], br.at[k],
            device_id=(lat, lon, peers[k]), device_id_type=MESH,
        )

    def weight_pass(k, which):
        origin = lax.rem(ch + n_ch - k, n_ch)
        part = pl.ds(2 * which, 2)
        return pltpu.make_async_remote_copy(
            wd.at[origin, part], wd.at[origin, part], vs.at[k], vr.at[k],
            device_id=(lat, partner, ch), device_id_type=MESH,
        )

    for k in range(1, n_ch):
        weight_send(k).start()
        bias_send(k).start()

    for pad, height in ((xp, 2), (hid, 4)):
        @pl.when(lat == 0)
        def _():
            pad[0:height] = jnp.zeros((height,) + pad.shape[1:], pad.dtype)

        @pl.when(lat == n_lat - 1)
        def _():
            pad[rows + height :] = jnp.zeros((height,) + pad.shape[1:], pad.dtype)

        @pl.when(lon == 0)
        def _():
            pad[:, 0:SIDE] = jnp.zeros((rows + 2 * height, SIDE, pad.shape[2]), pad.dtype)

        @pl.when(lon == n_lon - 1)
        def _():
            pad[:, cols + SIDE :] = jnp.zeros((rows + 2 * height, SIDE, pad.shape[2]), pad.dtype)

    span_cols = cols + 2 * SIDE

    def first(begin, count):
        total = None
        for tap in range(5):
            window = xp[pl.ds(begin + tap, count)].reshape(count * span_cols, width)
            term = lax.dot_general(
                window, w1[tap], (((1,), (1,)), ((), ())), preferred_element_type=jnp.float32
            )
            total = term if total is None else total + term
        total = total.reshape(count, span_cols, 5 * share)
        value = None
        for tap in range(5):
            low = SIDE - 2 + tap
            piece = total[:, low : low + cols, tap * share : (tap + 1) * share]
            value = piece if value is None else value + piece
        value = jax.nn.gelu(value + b1_ref[...][None], approximate=True)
        hid[pl.ds(begin + 4, count), pl.ds(SIDE, cols)] = value.astype(jnp.bfloat16)

    loads[0].wait()
    loads[1].wait()
    arrive(feature_halo, range(2))

    @pl.loop(0, (rows - 4) // 4)
    def _(step):
        first(2 + 4 * step, 4)

    arrive(feature_halo, range(2, 8))
    first(0, 2)
    first(rows - 2, 2)
    start(hidden_halo, range(8))

    def spread(begin, count):
        pieces = [
            hid[pl.ds(begin, count), pl.ds(SIDE - 4 + 2 * tap, cols)] for tap in range(5)
        ]
        cols_ref[pl.ds(begin, count)] = jnp.concatenate(pieces, axis=2)

    def second(block):
        total = None
        for tap in range(5):
            window = cols_ref[pl.ds(per * block + 2 * tap, per)].reshape(per * cols, 5 * share)
            term = jnp.dot(window, w2[tap], preferred_element_type=jnp.float32)
            total = term if total is None else total + term
        pb[block] = total.astype(jnp.bfloat16).reshape(per, cols, width)

    arrive(hidden_halo, range(2))
    loads[2].wait()

    @pl.loop(0, rows // 4)
    def _(step):
        spread(4 + 4 * step, 4)

    middle = n_ch // 2
    low = ch < middle
    across = jnp.where(low, middle, middle - 1)
    outer = jnp.where(low, n_ch - 1, 0)
    beside = jnp.where(low, middle - 1 - ch, n_ch + middle - 1 - ch)
    edge = jnp.logical_or(ch == 0, ch == n_ch - 1)
    inside = jnp.logical_not(edge)
    far = (across, outer)

    halves = [pl.ds(part * (per // 2), per // 2) for part in range(2)]

    def relay_copy(n, part):
        return pltpu.make_async_remote_copy(
            pb.at[far[n], halves[part]], via.at[n, halves[part]], rs.at[2 * n + part], rr.at[2 * n + part],
            device_id=(lat, lon, beside), device_id_type=MESH,
        )

    def far_copy(n, part):
        return pltpu.make_async_remote_copy(
            pb.at[far[n], halves[part]], got.at[ch, halves[part]], ps.at[2 * n + part], pr.at[ch],
            device_id=(lat, lon, far[n]), device_id_type=MESH,
        )

    def share_copy(block):
        return pltpu.make_async_remote_copy(
            pb.at[block], got.at[ch], ps.at[4], pr.at[ch],
            device_id=(lat, lon, block), device_id_type=MESH,
        )

    second(across)

    @pl.when(edge)
    def _():
        relay_copy(0, 0).start()
        relay_copy(0, 1).start()

    arrive(hidden_halo, range(2, 8))
    spread(0, 4)
    spread(rows + 4, 4)
    second(outer)

    @pl.when(edge)
    def _():
        relay_copy(1, 0).start()
        relay_copy(1, 1).start()

    second(beside)
    share_copy(beside).start()

    @pl.when(inside)
    def _():
        for n in range(2):
            for part in range(2):
                relay_copy(n, part).wait_recv()
                here = halves[part]
                both = pb[far[n], here].astype(jnp.float32) + via[n, here].astype(jnp.float32)
                pb[far[n], here] = both.astype(jnp.bfloat16)
                far_copy(n, part).start()

    second(ch)
    for k in range(1, n_ch):
        weight_send(k).wait_recv()
        weight_pass(k, half).start()


    mixed = xp[pl.ds(2 + per * ch, per), pl.ds(SIDE, cols)].astype(jnp.float32) + b2_ref[...][None]
    mixed = mixed + pb[ch].astype(jnp.float32)
    for origin in (beside, across):
        pltpu.make_async_remote_copy(
            pb.at[0], got.at[origin], ps.at[0], pr.at[origin],
            device_id=(lat, lon, origin), device_id_type=MESH,
        ).wait_recv()
        mixed = mixed + got[origin].astype(jnp.float32)
    mean = jnp.sum(mixed, axis=2, keepdims=True) / width
    variance = jnp.sum(mixed * mixed, axis=2, keepdims=True) / width - mean * mean
    normed = (mixed - mean) * lax.rsqrt(variance + 1e-05) * gain_ref[...][None] + shift_ref[...][None]
    normed = normed.astype(jnp.bfloat16).astype(jnp.float32).reshape(per * cols, width)
    for part in range(width // 128):
        nf[part] = normed[:, part * 128 : (part + 1) * 128]

    loads[3].wait()
    loads[4].wait()
    for k in range(1, n_ch):
        bias_send(k).wait_recv()
        weight_pass(k, 1 - half).wait_recv()

    result = None
    for tap in range(4):
        i, j = tap // 2, tap % 2
        picked = [
            jnp.concatenate(
                [
                    nf[part, pl.ds((2 * r + i) * cols + j, cols // 2, stride=2), :]
                    for part in range(width // 128)
                ],
                axis=1,
            )
            for r in range(per // 2)
        ]
        window = jnp.concatenate(picked, axis=0).astype(jnp.bfloat16)
        term = lax.dot_general(
            window, wd[:, tap].reshape(n_ch * share, width), (((1,), (1,)), ((), ())),
            preferred_element_type=jnp.float32,
        )
        result = term if result is None else result + term
    for to in range(n_ch):
        piece = result[:, to * share : (to + 1) * share] + bd[to]
        ob[to] = piece.astype(jnp.bfloat16).reshape(per // 2, cols // 2, share)

    def out_copy(k):
        place = pl.ds((per // 2) * ch, per // 2)
        return pltpu.make_async_remote_copy(
            ob.at[peers[k]], out_ref.at[place], os_.at[k], or_.at[k],
            device_id=(lat, lon, peers[k]), device_id_type=MESH,
        )

    own = pltpu.make_async_copy(ob.at[ch], out_ref.at[pl.ds((per // 2) * ch, per // 2)], local_sem.at[5])
    for k in range(1, n_ch):
        out_copy(k).start()
    own.start()

    drain(feature_halo, range(8))
    drain(hidden_halo, range(8))
    for k in range(1, n_ch):
        weight_send(k).wait_send()
        bias_send(k).wait_send()
        weight_pass(k, half).wait_send()
    share_copy(beside).wait_send()
    for n in range(2):
        @pl.when(edge)
        def _(n=n):
            relay_copy(n, 0).wait_send()
            relay_copy(n, 1).wait_send()

        @pl.when(inside)
        def _(n=n):
            far_copy(n, 0).wait_send()
            far_copy(n, 1).wait_send()
    own.wait()
    for k in range(1, n_ch):
        out_copy(k).wait_send()
        origin = lax.rem(ch + n_ch - k, n_ch)
        pltpu.make_async_remote_copy(
            ob.at[0], out_ref.at[pl.ds((per // 2) * origin, per // 2)], os_.at[k], or_.at[k],
            device_id=(lat, lon, peers[k]), device_id_type=MESH,
        ).wait_recv()


def body(counts, features, w_first, bias_first, w_second, bias_second, norm_gain, norm_shift, w_down, bias_down):
    _, rows, cols, width = features.shape
    n_ch = counts[2]
    share = w_first.shape[3]
    per = rows // n_ch
    bf16, f32 = jnp.bfloat16, jnp.float32
    dma = pltpu.SemaphoreType.DMA
    anywhere = pl.BlockSpec(memory_space=pl.ANY)
    vmem = pl.BlockSpec(memory_space=pltpu.VMEM)
    result = pl.pallas_call(
        functools.partial(kernel, counts),
        out_shape=jax.ShapeDtypeStruct((rows // 2, cols // 2, share), bf16),
        in_specs=[anywhere, anywhere, vmem, anywhere, vmem, vmem, vmem, anywhere, vmem],
        out_specs=anywhere,
        scratch_shapes=[
            pltpu.VMEM((rows + 4, cols + 2 * SIDE, width), bf16),
            pltpu.VMEM((rows + 8, cols + 2 * SIDE, share), bf16),
            pltpu.VMEM((rows + 8, cols, 5 * share), bf16),
            pltpu.VMEM((5, 5 * share, width), bf16),
            pltpu.VMEM((5, 5 * share, width), bf16),
            pltpu.VMEM((n_ch, 4, share, width), bf16),
            pltpu.VMEM((n_ch, 1, share), f32),
            pltpu.VMEM((n_ch, per, cols, width), bf16),
            pltpu.VMEM((n_ch, per, cols, width), bf16),
            pltpu.VMEM((2, per, cols, width), bf16),
            pltpu.VMEM((width // 128, per * cols, 128), f32),
            pltpu.VMEM((n_ch, per // 2, cols // 2, share), bf16),
            dma((6,)), dma((8,)), dma((8,)), dma((8,)), dma((8,)),
            dma((n_ch,)), dma((n_ch,)), dma((n_ch,)), dma((n_ch,)), dma((n_ch,)), dma((n_ch,)),
            dma((5,)), dma((n_ch,)), dma((4,)), dma((4,)), dma((n_ch,)), dma((n_ch,)),
        ],
        compiler_params=pltpu.CompilerParams(
            collective_id=0, has_side_effects=True, vmem_limit_bytes=60 * 1024 * 1024
        ),
        cost_estimate=pl.CostEstimate(flops=1700000000, bytes_accessed=3000000, transcendentals=70000),
    )(
        features[0],
        jnp.transpose(w_first, (0, 1, 3, 2)).reshape(5, 5 * share, width),
        bias_first.reshape(1, share),
        w_second.reshape(5, 5 * share, width),
        bias_second.reshape(1, width),
        norm_gain.reshape(1, width),
        norm_shift.reshape(1, width),
        jnp.transpose(w_down, (0, 1, 3, 2)).reshape(4, share, width),
        bias_down.reshape(1, share),
    )
    return result[None]


def solution(mesh):
    placed = (
        P(None, "lat", "lon", None),
        P(None, None, None, "ch"),
        P("ch"),
        P(None, None, "ch", None),
        P(),
        P(),
        P(),
        P(None, None, None, "ch"),
        P("ch"),
    )
    counts = tuple(mesh.shape[name] for name in ("lat", "lon", "ch"))
    return jax.shard_map(
        functools.partial(body, counts),
        mesh=mesh, in_specs=placed, out_specs=P(None, "lat", "lon", "ch"), check_vma=False,
    )
```
